32 devices in a mesh: dp: 4 (over z), expert: 8 (over y, x, core).
Axes of the slice: x: 2, y: 2, z: 4, core: 2. Of those that a mesh axis runs over, the one named last changes fastest.
Arguments:
- tokens: bfloat16 [1024, 2048], P(('dp', 'expert')), may hold values from -6 to 6
- norm_gain: float32 [2, 2048], replicated, may hold values from 0.5 to 1.5
- routes: int32 [2, 1024, 8], P(None, ('dp', 'expert')), may hold values from 0 to 31, all different within a row; in each aligned block of 32 rows (0 to 31, 32 to 63, ..., all dimensions but the last counted through in order) at most 12 rows name the same one
- gates: float32 [2, 1024, 8], P(None, ('dp', 'expert')), may hold values from 0.03 to 0.3
- placement: int32 [2, 32], replicated, may hold values from 0 to 31, each once within a row
- w_in: bfloat16 [2, 32, 2048, 1536], P(None, ('dp', 'expert')), may hold values from -0.125 to 0.125
- in_scale: float32 [2, 32, 16, 12], P(None, ('dp', 'expert')), may hold values from 0.5 to 2
- w_out: bfloat16 [2, 32, 768, 2048], P(None, ('dp', 'expert')), may hold values from -0.21875 to 0.21875
- out_scale: float32 [2, 32, 6, 16], P(None, ('dp', 'expert')), may hold values from 0.5 to 2
Outputs:
- stream: bfloat16 [1024, 2048], P(('dp', 'expert'))
The draws below stay inside these ranges and needn't reach their ends.
Inputs may be any that keep to these rules, and one draw needn't show every extreme that they name: `routes`: each token names 8 different experts in each layer; among the tokens of one device in one layer no expert is named more than 12 times, a bound that some block reaches. `placement`: each layer's row is a permutation of the experts; device position p is p's index along dp+expert, dp slowest.
All inputs are finite; a program needn't handle non-finite values.
Results may differ from the reference program's by a relative error of at most 0.009.
Values may be sent and summed in bfloat16 or wider, within the bound.
A program may use at most 128 MiB of HBM per device.

```python
import math
import jax
import jax.numpy as jnp
import numpy as np
from jax import lax

D = 2048
FF = 768
TOP = 8
QBLK = 128
LAYERS = 2
TOK_DEV = 32
EXPERTS = 32
TOKENS = 1024
CAP = 12


def levels(stream_key, shape, shards, smallest, largest):
    def one(axis_at, shards_of):
        draws = jax.random.uniform(jax.random.fold_in(jax.random.fold_in(stream_key, 6), axis_at), (shards_of,), jnp.float32, smallest / len(shards), largest / len(shards))
        return jnp.repeat(jnp.exp(draws), shape[axis_at] // shards_of).reshape((-1,) + (1,) * (len(shape) - axis_at - 1))

    gain = one(*shards[0])
    for cut in shards[1:]:
        gain = gain * one(*cut)
    return gain


def shared_out(rng, own, number, rows, count, top, most, lean):
    order = jax.random.permutation(rng, count)
    crowded, common = load_shares(count, rows * top, most, lean, True), load_shares(count, rows * top, most, lean, False)
    places = jnp.arange(count)

    def named(tallies, rotation):
        used = int((tallies > 0).sum())
        fixed = max(1, used // 4)
        shifted = fixed + (places - fixed + rotation * (used - fixed)) % max(1, count - fixed)
        return jnp.zeros((count,), jnp.int32).at[order[jnp.where(places < fixed, places, shifted)]].set(jnp.asarray(tallies, jnp.int32))

    tallies = jnp.where(number % 4 == 0, named(crowded, number // 4), named(common, number - number // 4 - 1))
    mixed = jax.random.permutation(jax.random.fold_in(own, 3), count)
    donor, taker = mixed[0:count // 2 * 2:2], mixed[1:count // 2 * 2:2]
    room = jnp.minimum(tallies[donor] - 1, most - tallies[taker]) // 2
    room = jnp.where((donor == order[0]) | (taker == order[0]) | (tallies[taker] == 0), 0, jnp.maximum(room, 0))
    shifted = jax.random.randint(jax.random.fold_in(own, 4), (count // 2,), 0, 1 << 20) % (room + 1)
    tallies = tallies.at[donor].add(-shifted).at[taker].add(shifted)
    labels = jnp.searchsorted(jnp.cumsum(tallies), jnp.arange(rows * top), side="right").astype(jnp.int32)
    table = labels.reshape(top, rows).T
    table = table[jax.random.permutation(jax.random.fold_in(own, 1), rows)]
    rotation = jax.random.randint(jax.random.fold_in(own, 2), (rows, 1), 0, top)
    return jnp.take_along_axis(table, (jnp.arange(top)[None, :] + rotation) % top, axis=1)


def load_shares(number_of, total, most, skew, full):
    weights = [(1 << 20) // math.isqrt(standing ** skew) + 1 for standing in range(1, number_of + 1)]
    largest = most if full else min(most, max(-(-total // number_of), total * weights[0] // sum(weights)))
    least = 1 if total - largest >= number_of - 1 else 0
    holding, rest = [largest] + [least] * (number_of - 1), total - largest - least * (number_of - 1)
    while rest > 0:
        movable = [i for i in range(1, number_of) if holding[i] < largest] or [i for i in range(1, number_of) if holding[i] < most]
        pool, remaining = sum([weights[i] for i in movable]), rest
        for i in movable:
            extra = min(most - holding[i], max(1, remaining * weights[i] // pool), rest)
            holding[i] = holding[i] + extra
            rest = rest - extra
    return np.array(holding)


def scatter_about(stream_key, shape, deviation, reach, split=(), kind=jnp.bfloat16):
    level = levels(stream_key, shape, split, -0.22, 0.18) if split else 1.0
    entries = jax.random.normal(stream_key, shape, jnp.float32) * deviation * level
    return jnp.minimum(jnp.maximum(entries, -reach), reach).astype(kind)


def setup_inputs(seed: int = 0) -> dict:
    arg_keys = jax.random.split(jax.random.key(seed), 10)
    tokens = scatter_about(arg_keys[0], (TOKENS, D), 1.0, 6.0, ((0, 32),))
    norm_gain = jnp.clip(jax.random.uniform(arg_keys[1], (LAYERS, D), jnp.float32, 0.5, 1.5), 0.5, 1.5)
    routes_keys = jax.random.split(jax.random.fold_in(arg_keys[2], 1), LAYERS * TOKENS // TOK_DEV)
    routes_turns = jax.random.permutation(jax.random.fold_in(arg_keys[2], 3), LAYERS * TOKENS // TOK_DEV)
    routes = jax.vmap(lambda own, number: shared_out(jax.random.fold_in(arg_keys[2], 2), own, number, TOK_DEV, EXPERTS, TOP, CAP, 2))(routes_keys, routes_turns).reshape((LAYERS, TOKENS, TOP))
    gates = jnp.clip(jnp.exp(math.log(0.3) - 2.3025852 * jax.random.uniform(arg_keys[3], (LAYERS, TOKENS, TOP), jnp.float32) ** levels(arg_keys[3], (LAYERS, TOKENS, TOP), ((1, 32),), -0.2, 0.2)), 0.03, 0.3)
    placement = jax.vmap(lambda own: jax.random.permutation(own, EXPERTS))(jax.random.split(arg_keys[4], LAYERS)).reshape((LAYERS, EXPERTS)).astype(jnp.int32)
    w_in = scatter_about(arg_keys[5], (LAYERS, EXPERTS, D, 2 * FF), D ** -0.5, 0.125, ((1, 32),))
    in_scale = jnp.clip(jnp.exp(math.log(2.0) - 1.3862944 * jax.random.uniform(arg_keys[6], (LAYERS, EXPERTS, D // QBLK, 2 * FF // QBLK), jnp.float32) ** levels(arg_keys[6], (LAYERS, EXPERTS, D // QBLK, 2 * FF // QBLK), ((1, 32),), -0.2, 0.2)), 0.5, 2.0)
    w_out = scatter_about(arg_keys[7], (LAYERS, EXPERTS, FF, D), FF ** -0.5, 0.21875, ((1, 32),))
    out_scale = jnp.clip(jnp.exp(math.log(2.0) - 1.3862944 * jax.random.uniform(arg_keys[8], (LAYERS, EXPERTS, FF // QBLK, D // QBLK), jnp.float32) ** levels(arg_keys[8], (LAYERS, EXPERTS, FF // QBLK, D // QBLK), ((1, 32),), -0.2, 0.2)), 0.5, 2.0)
    return {"tokens": tokens, "norm_gain": norm_gain, "routes": routes, "gates": gates, "placement": placement, "w_in": w_in, "in_scale": in_scale, "w_out": w_out, "out_scale": out_scale}


epsilon = 1e-06

def dequantize(quantized, scales, block_size):
    height, breadth = quantized.shape
    blocks = quantized.astype(jnp.float32).reshape(height // block_size, block_size, breadth // block_size, block_size)
    return (blocks * scales[:, None, :, None]).reshape(height, breadth).astype(jnp.bfloat16)

def reference(tokens, norm_gain, routes, gates, placement, w_in, in_scale, w_out, out_scale):
    stream = tokens
    assigned = TOK_DEV * TOP
    expert_ids = jnp.arange(EXPERTS, dtype=jnp.int32)
    for layer_index in range(LAYERS):
        stream_f = stream.astype(jnp.float32)
        normed = (stream_f * lax.rsqrt(lax.optimization_barrier(jnp.mean(stream_f * stream_f, axis=-1, keepdims=True)) + epsilon) * norm_gain[layer_index]).astype(jnp.bfloat16)
        holder = jnp.argsort(placement[layer_index]).astype(jnp.int32)
        chosen = routes[layer_index].reshape(EXPERTS, assigned).astype(jnp.int32)
        onehot = (chosen[:, :, None] == expert_ids[None, None, :]).astype(jnp.int32)
        ranks = lax.optimization_barrier(jnp.sum((jnp.cumsum(onehot, axis=1) - 1) * onehot, axis=2)).astype(jnp.int32)
        source = jnp.arange(EXPERTS, dtype=jnp.int32)[:, None]
        slot_rows = (source * CAP + ranks).reshape(-1).astype(jnp.int32)
        token_of = (source * TOK_DEV + jnp.arange(assigned, dtype=jnp.int32)[None, :] // TOP).reshape(-1).astype(jnp.int32)
        flat_expert = chosen.reshape(-1)
        table = jnp.full((EXPERTS, EXPERTS * CAP), TOKENS, jnp.int32).at[flat_expert, slot_rows].set(token_of)
        weight_table = jnp.zeros((EXPERTS, EXPERTS * CAP), jnp.float32).at[flat_expert, slot_rows].set(gates[layer_index].reshape(-1))
        padded = jnp.concatenate([normed, jnp.zeros((1, D), jnp.bfloat16)], axis=0)

        def expert_step(total, expert):
            holder_row = holder[expert]
            in_weight = dequantize(w_in[layer_index, holder_row], in_scale[layer_index, holder_row], QBLK)
            out_weight = dequantize(w_out[layer_index, holder_row], out_scale[layer_index, holder_row], QBLK)
            picked = table[expert]
            token_rows = padded[picked]
            gate_up = jnp.dot(token_rows, in_weight, preferred_element_type=jnp.float32)
            hidden = (jax.nn.silu(gate_up[:, :FF]) * gate_up[:, FF:]).astype(jnp.bfloat16)
            answer = jnp.dot(hidden, out_weight, preferred_element_type=jnp.float32).astype(jnp.bfloat16)
            total = total.at[picked].add(weight_table[expert][:, None] * answer.astype(jnp.float32))
            return (total, None)
        total, _ = lax.scan(expert_step, jnp.zeros((TOKENS + 1, D), jnp.float32), expert_ids)
        stream = (stream_f + total[:TOKENS]).astype(jnp.bfloat16)
    return stream
```

```python
import functools

import jax
import jax.numpy as jnp
from jax import lax
from jax.experimental import pallas as pl
from jax.experimental.pallas import tpu as pltpu
from jax.sharding import PartitionSpec as P

MESH = pl.DeviceIdType.MESH

QBLK = 128


epsilon = 1e-06


def dequantize(quantized, scales, block_size):
    widened = jnp.repeat(jnp.repeat(scales, block_size, axis=0), block_size, axis=1)
    return (quantized.astype(jnp.float32) * widened).astype(jnp.bfloat16)


def shards(tokens, norm_gain, routes, gates, placement, w_in, in_scale, w_out, out_scale):
    tok_count = tokens.shape[0]
    width = tokens.shape[1]
    fanout = routes.shape[2]
    experts_all = placement.shape[1]
    capacity = max(2, 3 * tok_count * fanout // (2 * experts_all))
    hidden_width = w_out.shape[2]
    expert_ids = jnp.arange(experts_all, dtype=jnp.int32)
    slot_ids = jnp.arange(experts_all * capacity, dtype=jnp.int32)
    stream = tokens
    for layer_index in range(w_in.shape[0]):
        stream_f = stream.astype(jnp.float32)
        normed = (
            stream_f
            * lax.rsqrt(jnp.mean(stream_f * stream_f, axis=-1, keepdims=True) + epsilon)
            * norm_gain[layer_index]
        ).astype(jnp.bfloat16)
        in_weight = dequantize(w_in[layer_index, 0], in_scale[layer_index, 0], QBLK)
        out_weight = dequantize(w_out[layer_index, 0], out_scale[layer_index, 0], QBLK)
        matches = (placement[layer_index][:, None] == expert_ids[None, :]).astype(jnp.int32)
        holder = jnp.sum(matches * expert_ids[:, None], axis=0)
        chosen = routes[layer_index].reshape(-1)
        onehot = (chosen[:, None] == expert_ids[None, :]).astype(jnp.int32)
        ranks = jnp.sum((jnp.cumsum(onehot, axis=0) - 1) * onehot, axis=1)
        target = jnp.sum(onehot * holder[None, :], axis=1)
        slot_rows = target * capacity + ranks
        selector = (slot_rows[:, None] == slot_ids[None, :]).astype(jnp.bfloat16)
        spread = jnp.sum(
            selector.reshape(tok_count, fanout, -1).astype(jnp.float32), axis=1
        ).astype(jnp.bfloat16)
        outgoing = lax.dot_general(
            spread, normed, (((0,), (0,)), ((), ())), preferred_element_type=jnp.float32
        ).astype(jnp.bfloat16)
        outgoing = outgoing.reshape(experts_all, capacity, width)
        arrived = lax.all_to_all(
            outgoing, ("dp", "expert"), split_axis=0, concat_axis=0, tiled=True
        )
        arrived_shape = arrived.shape
        token_rows = arrived.reshape(-1, width)
        gate_up = jnp.dot(token_rows, in_weight, preferred_element_type=jnp.float32)
        hidden = (jax.nn.silu(gate_up[:, :hidden_width]) * gate_up[:, hidden_width:]).astype(
            jnp.bfloat16
        )
        answer = jnp.dot(hidden, out_weight, preferred_element_type=jnp.float32).astype(
            jnp.bfloat16
        )
        returned = lax.all_to_all(
            answer.reshape(arrived_shape), ("dp", "expert"), split_axis=0, concat_axis=0, tiled=True
        )
        back_rows = jnp.dot(
            selector, returned.reshape(-1, width), preferred_element_type=jnp.float32
        )
        back_rows = back_rows.reshape(tok_count, fanout, width)
        mixed = jnp.sum(back_rows * gates[layer_index][:, :, None], axis=1)
        stream = (stream_f + mixed).astype(jnp.bfloat16)
    return stream


GZ, GX, GY, GA, GB, GC, RC, RA, RB, RX, RY, RZ = range(12)


def moe_kernel(
    layers, experts_all, tok_ref, gain_ref, wts_ref, isc_ref, osc_ref, win_hbm, wout_hbm, out_ref,
    rows, win, wout, hid, part, acc, core_in, diag_out, diag_in, side_out, side_in, z_out, z_in,
    w_sem, send_sem, recv_sem,
):
    count, width = tok_ref.shape
    full = width + 128
    half = width // 2
    ff = wout.shape[1]
    z = lax.axis_index("dp")
    e = lax.axis_index("expert")
    c = e % 2
    q = e // 2
    x = q % 2
    y = q // 2
    xq = q + 1 - 2 * x
    yq = q + 2 - 4 * y
    dq = 3 - q
    dev_x = (z, e + 2 - 4 * x)
    dev_y = (z, e + 4 - 8 * y)
    dev_c = (z, e + 1 - 2 * c)

    def plane(k):
        return (z % 2 + k % 2) % 2 + 2 * ((z // 2 + k // 2) % 2)

    for l in range(layers):
        pltpu.make_async_copy(win_hbm.at[l, 0], win.at[l], w_sem.at[l, 0]).start()
        pltpu.make_async_copy(wout_hbm.at[l, 0], wout.at[l], w_sem.at[l, 1]).start()

    barrier = pltpu.get_barrier_semaphore()
    partners = [dev_x, dev_y, dev_c] + [(plane(k), e) for k in range(1, 4)]
    for dev in partners:
        pl.semaphore_signal(barrier, inc=1, device_id=dev, device_id_type=MESH)
    pl.semaphore_wait(barrier, len(partners))

    def scale_in(l, lo, hi):
        @pl.loop(lo * 4, hi * 4)
        def _(i):
            r = pl.ds(pl.multiple_of(i * 32, 32), 32)
            win[l, r, :] = (win[l, r, :].astype(jnp.float32) * isc_ref[l, i // 4]).astype(jnp.bfloat16)

    def scale_out(l):
        @pl.loop(0, ff // 32)
        def _(i):
            r = pl.ds(pl.multiple_of(i * 32, 32), 32)
            wout[l, r, :] = (wout[l, r, :].astype(jnp.float32) * osc_ref[l, i // 4]).astype(jnp.bfloat16)

    blocks = win.shape[1] // QBLK

    def dequant(l, step):
        if step == 0:
            pltpu.make_async_copy(win_hbm.at[l, 0], win.at[l], w_sem.at[l, 0]).wait()
            scale_in(l, 0, blocks // 2)
        elif step == 1:
            scale_in(l, blocks // 2, blocks)
        else:
            pltpu.make_async_copy(wout_hbm.at[l, 0], wout.at[l], w_sem.at[l, 1]).wait()
            scale_out(l)

    acc[...] = tok_ref[...].astype(jnp.float32)

    def layer(l, carry):
        sent = []

        def copy(src, dst, k, kind, dev):
            return pltpu.make_async_remote_copy(
                src_ref=src, dst_ref=dst,
                send_sem=send_sem.at[l, k, kind], recv_sem=recv_sem.at[l, k, kind],
                device_id=dev, device_id_type=MESH,
            )

        def start(src, dst, k, kind, dev):
            op = copy(src, dst, k, kind, dev)
            op.start()
            sent.append(op)

        def arrived(dst, k, kind, dev):
            copy(dst, dst, k, kind, dev).wait_recv()

        left, right = pl.ds(0, half), pl.ds(half, full - half)

        def shard(k, place):
            return rows.at[l, plane(k), c, place]

        def g1(k):
            mine = shard(k, q)
            if k > 0:
                arrived(mine, k, GZ, (plane(k), e))
            start(mine, mine, k, GX, dev_x)
            start(mine, mine, k, GY, dev_y)

        def g2(k):
            arrived(shard(k, xq), k, GX, dev_x)
            piece = rows.at[l, plane(k), c, xq, :, left]
            start(piece, piece, k, GA, dev_y)
            arrived(shard(k, yq), k, GY, dev_y)
            piece = rows.at[l, plane(k), c, yq, :, right]
            start(piece, piece, k, GB, dev_x)

        def g3(k):
            arrived(rows.at[l, plane(k), c, dq, :, left], k, GA, dev_y)
            arrived(rows.at[l, plane(k), c, dq, :, right], k, GB, dev_x)
            ours = rows.at[l, plane(k), c]
            start(ours, ours, k, GC, dev_c)

        def compute(k):
            arrived(rows.at[l, plane(k), 1 - c], k, GC, dev_c)
            zk = plane(k)
            total = 8 * count
            picks = rows[l, zk, :, :, :, width:].reshape(total, full - width).astype(jnp.float32)
            lane = lax.broadcasted_iota(jnp.int32, picks.shape, 1)
            me = z * 8 + e
            own = (lane == me) | (lane == me + experts_all)
            weight = jnp.sum(jnp.where(own, picks, 0.0), axis=1, keepdims=True)

            @pl.loop(0, ff // 256)
            def _(j):
                data = rows[l, zk, :, :, :, :width].reshape(total, width)
                g_cols = pl.ds(pl.multiple_of(j * 256, 256), 256)
                u_cols = pl.ds(pl.multiple_of(ff + j * 256, 256), 256)
                gate = jnp.dot(data, win[l, :, g_cols], preferred_element_type=jnp.float32)
                up = jnp.dot(data, win[l, :, u_cols], preferred_element_type=jnp.float32)
                hid[:, g_cols] = (gate / (1.0 + jnp.exp(-gate)) * up).astype(jnp.bfloat16)

            @pl.loop(0, width // 512)
            def _(j):
                cols = pl.ds(pl.multiple_of(j * 512, 512), 512)
                answer = jnp.dot(hid[...], wout[l, :, cols], preferred_element_type=jnp.float32)
                answer = answer.astype(jnp.bfloat16).astype(jnp.float32) * weight
                part[k, :, :, :, cols] = answer.astype(jnp.bfloat16).reshape(2, 4, count, 512)

            start(part.at[k, 1 - c], core_in.at[l, k], k, RC, dev_c)

        def chip_sum(k, place):
            return part[k, c, place].astype(jnp.float32) + core_in[l, k, place].astype(jnp.float32)

        def r2(k):
            arrived(core_in.at[l, k], k, RC, dev_c)
            far = chip_sum(k, dq).astype(jnp.bfloat16)
            diag_out[k, 0] = far[:, :half]
            diag_out[k, 1] = far[:, half:]
            start(diag_out.at[k, 0], diag_in.at[l, k, 0], k, RA, dev_x)
            start(diag_out.at[k, 1], diag_in.at[l, k, 1], k, RB, dev_y)

        def r3(k):
            arrived(diag_in.at[l, k, 1], k, RB, dev_y)
            near = chip_sum(k, xq)
            side_out[k, 0, :, :half] = near[:, :half].astype(jnp.bfloat16)
            side_out[k, 0, :, half:] = (near[:, half:] + diag_in[l, k, 1].astype(jnp.float32)).astype(jnp.bfloat16)
            start(side_out.at[k, 0], side_in.at[l, k, 0], k, RX, dev_x)
            arrived(diag_in.at[l, k, 0], k, RA, dev_x)
            near = chip_sum(k, yq)
            side_out[k, 1, :, :half] = (near[:, :half] + diag_in[l, k, 0].astype(jnp.float32)).astype(jnp.bfloat16)
            side_out[k, 1, :, half:] = near[:, half:].astype(jnp.bfloat16)
            start(side_out.at[k, 1], side_in.at[l, k, 1], k, RY, dev_y)

        def r4(k):
            arrived(side_in.at[l, k, 0], k, RX, dev_x)
            arrived(side_in.at[l, k, 1], k, RY, dev_y)
            whole = chip_sum(k, q) + side_in[l, k, 0].astype(jnp.float32) + side_in[l, k, 1].astype(jnp.float32)
            if k == 0:
                acc[...] += whole
            else:
                z_out[k] = whole.astype(jnp.bfloat16)
                start(z_out.at[k], z_in.at[l, k], k, RZ, (plane(k), e))

        stream = acc[...]
        inverse = lax.rsqrt(jnp.mean(stream * stream, axis=-1, keepdims=True) + epsilon)
        rows[l, z, c, q, :, :width] = (stream * inverse * gain_ref[l]).astype(jnp.bfloat16)
        rows[l, z, c, q, :, width:] = wts_ref[l]
        mine = rows.at[l, z, c, q]
        g1(0)
        for k in range(1, 4):
            start(mine, mine, k, GZ, (plane(k), e))

        def ahead(step):
            @pl.when(l + 1 < layers)
            def _():
                dequant(l + 1, step)

        @pl.when(l == 0)
        def _():
            dequant(0, 0)

        g2(0), g1(1)

        @pl.when(l == 0)
        def _():
            dequant(0, 1)

        g3(0), g2(1), g1(2)

        @pl.when(l == 0)
        def _():
            dequant(0, 2)

        compute(0), g3(1), g2(2), g1(3)
        compute(1), r2(0), g3(2), g2(3)
        compute(2), r3(0), r2(1), g3(3)
        compute(3), r4(0), r3(1), r2(2)
        ahead(0)
        r4(1), r3(2), r2(3)
        ahead(1)
        r4(2), r3(3)
        ahead(2)
        r4(3)
        for k in range(1, 4):
            arrived(z_in.at[l, k], k, RZ, (plane(k), e))
            acc[...] += z_in[l, k].astype(jnp.float32)
        acc[...] = acc[...].astype(jnp.bfloat16).astype(jnp.float32)
        for op in sent:
            op.wait_send()
        return carry

    lax.fori_loop(0, layers, layer, 0)
    out_ref[...] = acc[...].astype(jnp.bfloat16)


def fused(tokens, norm_gain, routes, gates, placement, w_in, in_scale, w_out, out_scale):
    count, width = tokens.shape
    layers = w_in.shape[0]
    ff = w_out.shape[2]
    chosen = routes[:, :, :, None] == placement[:, None, None, :]
    share = jnp.sum(jnp.where(chosen, gates[:, :, :, None], 0.0), axis=2)
    high = lax.reduce_precision(share, 8, 7)
    low = share - high
    wts = jnp.concatenate([high, low, jnp.zeros_like(high), jnp.zeros_like(high)], axis=-1)
    wts = wts.astype(jnp.bfloat16)
    isc = jnp.repeat(in_scale[:, 0], QBLK, axis=2)[:, :, None, :]
    osc = jnp.repeat(out_scale[:, 0], QBLK, axis=2)[:, :, None, :]
    gain = norm_gain[:, None, :]
    vmem = pl.BlockSpec(memory_space=pltpu.VMEM)
    hbm = pl.BlockSpec(memory_space=pl.ANY)
    b16 = jnp.bfloat16
    return pl.pallas_call(
        functools.partial(moe_kernel, layers, placement.shape[1]),
        out_shape=jax.ShapeDtypeStruct((count, width), b16),
        in_specs=[vmem] * 5 + [hbm] * 2,
        out_specs=vmem,
        scratch_shapes=[
            pltpu.VMEM((layers, 4, 2, 4, count, width + 128), b16),
            pltpu.VMEM((layers, width, 2 * ff), b16),
            pltpu.VMEM((layers, ff, width), b16),
            pltpu.VMEM((8 * count, ff), b16),
            pltpu.VMEM((4, 2, 4, count, width), b16),
            pltpu.VMEM((count, width), jnp.float32),
            pltpu.VMEM((layers, 4, 4, count, width), b16),
            pltpu.VMEM((4, 2, count, width // 2), b16),
            pltpu.VMEM((layers, 4, 2, count, width // 2), b16),
            pltpu.VMEM((4, 2, count, width), b16),
            pltpu.VMEM((layers, 4, 2, count, width), b16),
            pltpu.VMEM((4, count, width), b16),
            pltpu.VMEM((layers, 4, count, width), b16),
            pltpu.SemaphoreType.DMA((layers, 2)),
            pltpu.SemaphoreType.DMA((layers, 4, 12)),
            pltpu.SemaphoreType.DMA((layers, 4, 12)),
        ],
        compiler_params=pltpu.CompilerParams(
            collective_id=0, has_side_effects=True, vmem_limit_bytes=58 * 1024 * 1024
        ),
    )(tokens, gain, wts, isc, osc, w_in, w_out)


def solution(mesh):
    fits = mesh.shape["dp"] == 4 and mesh.shape["expert"] == 8
    return jax.shard_map(
        fused if fits else shards,
        mesh=mesh,
        in_specs=(
            P(("dp", "expert"), None),
            P(),
            P(None, ("dp", "expert"), None),
            P(None, ("dp", "expert"), None),
            P(),
            P(None, ("dp", "expert"), None, None),
            P(None, ("dp", "expert"), None, None),
            P(None, ("dp", "expert"), None, None),
            P(None, ("dp", "expert"), None, None),
        ),
        out_specs=P(("dp", "expert"), None),
        check_vma=False,
    )
```

```python
import functools

import jax
import jax.numpy as jnp
from jax import lax
from jax.experimental import pallas as pl
from jax.experimental.pallas import tpu as pltpu
from jax.sharding import PartitionSpec as P

MESH = pl.DeviceIdType.MESH

QBLK = 128


epsilon = 1e-06


def dequantize(quantized, scales, block_size):
    widened = jnp.repeat(jnp.repeat(scales, block_size, axis=0), block_size, axis=1)
    return (quantized.astype(jnp.float32) * widened).astype(jnp.bfloat16)


def shards(tokens, norm_gain, routes, gates, placement, w_in, in_scale, w_out, out_scale):
    tok_count = tokens.shape[0]
    width = tokens.shape[1]
    fanout = routes.shape[2]
    experts_all = placement.shape[1]
    capacity = max(2, 3 * tok_count * fanout // (2 * experts_all))
    hidden_width = w_out.shape[2]
    expert_ids = jnp.arange(experts_all, dtype=jnp.int32)
    slot_ids = jnp.arange(experts_all * capacity, dtype=jnp.int32)
    stream = tokens
    for layer_index in range(w_in.shape[0]):
        stream_f = stream.astype(jnp.float32)
        normed = (
            stream_f
            * lax.rsqrt(jnp.mean(stream_f * stream_f, axis=-1, keepdims=True) + epsilon)
            * norm_gain[layer_index]
        ).astype(jnp.bfloat16)
        in_weight = dequantize(w_in[layer_index, 0], in_scale[layer_index, 0], QBLK)
        out_weight = dequantize(w_out[layer_index, 0], out_scale[layer_index, 0], QBLK)
        matches = (placement[layer_index][:, None] == expert_ids[None, :]).astype(jnp.int32)
        holder = jnp.sum(matches * expert_ids[:, None], axis=0)
        chosen = routes[layer_index].reshape(-1)
        onehot = (chosen[:, None] == expert_ids[None, :]).astype(jnp.int32)
        ranks = jnp.sum((jnp.cumsum(onehot, axis=0) - 1) * onehot, axis=1)
        target = jnp.sum(onehot * holder[None, :], axis=1)
        slot_rows = target * capacity + ranks
        selector = (slot_rows[:, None] == slot_ids[None, :]).astype(jnp.bfloat16)
        spread = jnp.sum(
            selector.reshape(tok_count, fanout, -1).astype(jnp.float32), axis=1
        ).astype(jnp.bfloat16)
        outgoing = lax.dot_general(
            spread, normed, (((0,), (0,)), ((), ())), preferred_element_type=jnp.float32
        ).astype(jnp.bfloat16)
        outgoing = outgoing.reshape(experts_all, capacity, width)
        arrived = lax.all_to_all(
            outgoing, ("dp", "expert"), split_axis=0, concat_axis=0, tiled=True
        )
        arrived_shape = arrived.shape
        token_rows = arrived.reshape(-1, width)
        gate_up = jnp.dot(token_rows, in_weight, preferred_element_type=jnp.float32)
        hidden = (jax.nn.silu(gate_up[:, :hidden_width]) * gate_up[:, hidden_width:]).astype(
            jnp.bfloat16
        )
        answer = jnp.dot(hidden, out_weight, preferred_element_type=jnp.float32).astype(
            jnp.bfloat16
        )
        returned = lax.all_to_all(
            answer.reshape(arrived_shape), ("dp", "expert"), split_axis=0, concat_axis=0, tiled=True
        )
        back_rows = jnp.dot(
            selector, returned.reshape(-1, width), preferred_element_type=jnp.float32
        )
        back_rows = back_rows.reshape(tok_count, fanout, width)
        mixed = jnp.sum(back_rows * gates[layer_index][:, :, None], axis=1)
        stream = (stream_f + mixed).astype(jnp.bfloat16)
    return stream


GZ, GX, GY, GA, GB, GC, RC, RA, RB, RX, RY, RZ = range(12)


def moe_kernel(
    layers, experts_all, tok_ref, gain_ref, wts_ref, isc_ref, osc_ref, win_hbm, wout_hbm, out_ref,
    rows, win, wout, hid, part, acc, core_in, diag_out, diag_in, side_out, side_in, z_out, z_in,
    w_sem, send_sem, recv_sem,
):
    count, width = tok_ref.shape
    full = width + 128
    half = width // 2
    ff = wout.shape[1]
    z = lax.axis_index("dp")
    e = lax.axis_index("expert")
    c = e % 2
    q = e // 2
    x = q % 2
    y = q // 2
    xq = q + 1 - 2 * x
    yq = q + 2 - 4 * y
    dq = 3 - q
    dev_x = (z, e + 2 - 4 * x)
    dev_y = (z, e + 4 - 8 * y)
    dev_c = (z, e + 1 - 2 * c)

    def plane(k):
        return (z % 2 + k % 2) % 2 + 2 * ((z // 2 + k // 2) % 2)

    for l in range(layers):
        pltpu.make_async_copy(win_hbm.at[l, 0], win.at[l], w_sem.at[l, 0]).start()
        pltpu.make_async_copy(wout_hbm.at[l, 0], wout.at[l], w_sem.at[l, 1]).start()

    barrier = pltpu.get_barrier_semaphore()
    partners = [dev_x, dev_y, dev_c] + [(plane(k), e) for k in range(1, 4)]
    for dev in partners:
        pl.semaphore_signal(barrier, inc=1, device_id=dev, device_id_type=MESH)
    pl.semaphore_wait(barrier, len(partners))

    def scale_in(l, lo, hi):
        @pl.loop(lo * 4, hi * 4)
        def _(i):
            r = pl.ds(pl.multiple_of(i * 32, 32), 32)
            win[l, r, :] = (win[l, r, :].astype(jnp.float32) * isc_ref[l, pl.ds(i // 4, 1), :]).astype(jnp.bfloat16)

    def scale_out(l):
        @pl.loop(0, ff // 32)
        def _(i):
            r = pl.ds(pl.multiple_of(i * 32, 32), 32)
            wout[l, r, :] = (wout[l, r, :].astype(jnp.float32) * osc_ref[l, pl.ds(i // 4, 1), :]).astype(jnp.bfloat16)

    blocks = win.shape[1] // QBLK

    def dequant(l, step):
        if step == 0:
            pltpu.make_async_copy(win_hbm.at[l, 0], win.at[l], w_sem.at[l, 0]).wait()
            scale_in(l, 0, blocks // 2)
        elif step == 1:
            scale_in(l, blocks // 2, blocks)
        else:
            pltpu.make_async_copy(wout_hbm.at[l, 0], wout.at[l], w_sem.at[l, 1]).wait()
            scale_out(l)

    acc[...] = tok_ref[...].astype(jnp.float32)

    def layer(l, carry):
        sent = []

        def copy(src, dst, k, kind, dev):
            return pltpu.make_async_remote_copy(
                src_ref=src, dst_ref=dst,
                send_sem=send_sem.at[l, k, kind], recv_sem=recv_sem.at[l, k, kind],
                device_id=dev, device_id_type=MESH,
            )

        def start(src, dst, k, kind, dev):
            op = copy(src, dst, k, kind, dev)
            op.start()
            sent.append(op)

        def arrived(dst, k, kind, dev):
            copy(dst, dst, k, kind, dev).wait_recv()

        left, right = pl.ds(0, half), pl.ds(half, full - half)

        def shard(k, place):
            return rows.at[l, plane(k), c, place]

        def g1(k):
            mine = shard(k, q)
            if k > 0:
                arrived(mine, k, GZ, (plane(k), e))
            start(mine, mine, k, GX, dev_x)
            start(mine, mine, k, GY, dev_y)

        def g2(k):
            arrived(shard(k, xq), k, GX, dev_x)
            piece = rows.at[l, plane(k), c, xq, :, left]
            start(piece, piece, k, GA, dev_y)
            arrived(shard(k, yq), k, GY, dev_y)
            piece = rows.at[l, plane(k), c, yq, :, right]
            start(piece, piece, k, GB, dev_x)

        def g3(k):
            arrived(rows.at[l, plane(k), c, dq, :, left], k, GA, dev_y)
            arrived(rows.at[l, plane(k), c, dq, :, right], k, GB, dev_x)
            ours = rows.at[l, plane(k), c]
            start(ours, ours, k, GC, dev_c)

        def expand(k):
            arrived(rows.at[l, plane(k), 1 - c], k, GC, dev_c)
            zk = plane(k)
            total = 8 * count

            @pl.loop(0, ff // 256)
            def _(j):
                data = rows[l, zk, :, :, :, :width].reshape(total, width)
                g_cols = pl.ds(pl.multiple_of(j * 256, 256), 256)
                u_cols = pl.ds(pl.multiple_of(ff + j * 256, 256), 256)
                gate = jnp.dot(data, win[l, :, g_cols], preferred_element_type=jnp.float32)
                up = jnp.dot(data, win[l, :, u_cols], preferred_element_type=jnp.float32)
                hid[:, g_cols] = (gate / (1.0 + jnp.exp(-gate)) * up).astype(jnp.bfloat16)

        def contract(k):
            zk = plane(k)
            total = 8 * count
            picks = rows[l, zk, :, :, :, width:].reshape(total, full - width).astype(jnp.float32)
            lane = lax.broadcasted_iota(jnp.int32, picks.shape, 1)
            me = z * 8 + e
            own = (lane == me) | (lane == me + experts_all)
            weight = jnp.sum(jnp.where(own, picks, 0.0), axis=1, keepdims=True)

            @pl.loop(0, width // 512)
            def _(j):
                cols = pl.ds(pl.multiple_of(j * 512, 512), 512)
                answer = jnp.dot(hid[...], wout[l, :, cols], preferred_element_type=jnp.float32)
                answer = answer.astype(jnp.bfloat16).astype(jnp.float32) * weight
                part[k, :, :, :, cols] = answer.astype(jnp.bfloat16).reshape(2, 4, count, 512)

            start(part.at[k, 1 - c], core_in.at[l, k], k, RC, dev_c)

        def chip_sum(k, place):
            return part[k, c, place].astype(jnp.float32) + core_in[l, k, place].astype(jnp.float32)

        def r2(k):
            arrived(core_in.at[l, k], k, RC, dev_c)
            far = chip_sum(k, dq).astype(jnp.bfloat16)
            diag_out[k, 0] = far[:, :half]
            diag_out[k, 1] = far[:, half:]
            start(diag_out.at[k, 0], diag_in.at[l, k, 0], k, RA, dev_x)
            start(diag_out.at[k, 1], diag_in.at[l, k, 1], k, RB, dev_y)

        def r3(k):
            arrived(diag_in.at[l, k, 1], k, RB, dev_y)
            near = chip_sum(k, xq)
            side_out[k, 0, :, :half] = near[:, :half].astype(jnp.bfloat16)
            side_out[k, 0, :, half:] = (near[:, half:] + diag_in[l, k, 1].astype(jnp.float32)).astype(jnp.bfloat16)
            start(side_out.at[k, 0], side_in.at[l, k, 0], k, RX, dev_x)
            arrived(diag_in.at[l, k, 0], k, RA, dev_x)
            near = chip_sum(k, yq)
            side_out[k, 1, :, :half] = (near[:, :half] + diag_in[l, k, 0].astype(jnp.float32)).astype(jnp.bfloat16)
            side_out[k, 1, :, half:] = near[:, half:].astype(jnp.bfloat16)
            start(side_out.at[k, 1], side_in.at[l, k, 1], k, RY, dev_y)

        def r4(k):
            arrived(side_in.at[l, k, 0], k, RX, dev_x)
            arrived(side_in.at[l, k, 1], k, RY, dev_y)
            whole = chip_sum(k, q) + side_in[l, k, 0].astype(jnp.float32) + side_in[l, k, 1].astype(jnp.float32)
            if k == 0:
                acc[...] += whole
            else:
                z_out[k] = whole.astype(jnp.bfloat16)
                start(z_out.at[k], z_in.at[l, k], k, RZ, (plane(k), e))

        stream = acc[...]
        inverse = lax.rsqrt(jnp.mean(stream * stream, axis=-1, keepdims=True) + epsilon)
        rows[l, z, c, q, :, :width] = (stream * inverse * gain_ref[pl.ds(l, 1), :]).astype(jnp.bfloat16)
        rows[l, z, c, q, :, width:] = wts_ref[l]
        mine = rows.at[l, z, c, q]
        g1(0)
        for k in range(1, 4):
            start(mine, mine, k, GZ, (plane(k), e))

        def ahead(step):
            @pl.when(l + 1 < layers)
            def _():
                dequant(l + 1, step)

        @pl.when(l == 0)
        def _():
            dequant(0, 0)

        g2(0), g1(1)
        dequant(l, 1)
        g3(0), g2(1)
        dequant(l, 2)
        expand(0), g1(2), g3(1)
        contract(0), g2(2), g1(3)
        expand(1), r2(0), g3(2), g2(3)
        contract(1), r3(0), g3(3)
        expand(2), r4(0), r2(1)
        contract(2), r3(1)
        expand(3), r4(1), r2(2)
        contract(3), r3(2)
        ahead(0)
        r2(3), r4(2), r3(3), r4(3)
        for k in range(1, 4):
            arrived(z_in.at[l, k], k, RZ, (plane(k), e))
            acc[...] += z_in[l, k].astype(jnp.float32)
        acc[...] = acc[...].astype(jnp.bfloat16).astype(jnp.float32)
        for op in sent:
            op.wait_send()
        return carry

    lax.fori_loop(0, layers, layer, 0)
    out_ref[...] = acc[...].astype(jnp.bfloat16)


def fused(tokens, norm_gain, routes, gates, placement, w_in, in_scale, w_out, out_scale):
    count, width = tokens.shape
    layers = w_in.shape[0]
    ff = w_out.shape[2]
    chosen = routes[:, :, :, None] == placement[:, None, None, :]
    share = jnp.sum(jnp.where(chosen, gates[:, :, :, None], 0.0), axis=2)
    high = lax.reduce_precision(share, 8, 7)
    low = share - high
    wts = jnp.concatenate([high, low, jnp.zeros_like(high), jnp.zeros_like(high)], axis=-1)
    wts = wts.astype(jnp.bfloat16)
    isc = jnp.repeat(in_scale[:, 0], QBLK, axis=2)
    osc = jnp.repeat(out_scale[:, 0], QBLK, axis=2)
    vmem = pl.BlockSpec(memory_space=pltpu.VMEM)
    hbm = pl.BlockSpec(memory_space=pl.ANY)
    b16 = jnp.bfloat16
    return pl.pallas_call(
        functools.partial(moe_kernel, layers, placement.shape[1]),
        out_shape=jax.ShapeDtypeStruct((count, width), b16),
        in_specs=[vmem] * 5 + [hbm] * 2,
        out_specs=vmem,
        scratch_shapes=[
            pltpu.VMEM((layers, 4, 2, 4, count, width + 128), b16),
            pltpu.VMEM((layers, width, 2 * ff), b16),
            pltpu.VMEM((layers, ff, width), b16),
            pltpu.VMEM((8 * count, ff), b16),
            pltpu.VMEM((4, 2, 4, count, width), b16),
            pltpu.VMEM((count, width), jnp.float32),
            pltpu.VMEM((layers, 4, 4, count, width), b16),
            pltpu.VMEM((4, 2, count, width // 2), b16),
            pltpu.VMEM((layers, 4, 2, count, width // 2), b16),
            pltpu.VMEM((4, 2, count, width), b16),
            pltpu.VMEM((layers, 4, 2, count, width), b16),
            pltpu.VMEM((4, count, width), b16),
            pltpu.VMEM((layers, 4, count, width), b16),
            pltpu.SemaphoreType.DMA((layers, 2)),
            pltpu.SemaphoreType.DMA((layers, 4, 12)),
            pltpu.SemaphoreType.DMA((layers, 4, 12)),
        ],
        compiler_params=pltpu.CompilerParams(
            collective_id=0, has_side_effects=True, vmem_limit_bytes=58 * 1024 * 1024
        ),
    )(tokens, norm_gain, wts, isc, osc, w_in, w_out)


def solution(mesh):
    fits = mesh.shape["dp"] == 4 and mesh.shape["expert"] == 8
    return jax.shard_map(
        fused if fits else shards,
        mesh=mesh,
        in_specs=(
            P(("dp", "expert"), None),
            P(),
            P(None, ("dp", "expert"), None),
            P(None, ("dp", "expert"), None),
            P(),
            P(None, ("dp", "expert"), None, None),
            P(None, ("dp", "expert"), None, None),
            P(None, ("dp", "expert"), None, None),
            P(None, ("dp", "expert"), None, None),
        ),
        out_specs=P(("dp", "expert"), None),
        check_vma=False,
    )
```

```python
import functools

import jax
import jax.numpy as jnp
from jax import lax
from jax.experimental import pallas as pl
from jax.experimental.pallas import tpu as pltpu
from jax.sharding import PartitionSpec as P

MESH = pl.DeviceIdType.MESH

QBLK = 128


epsilon = 1e-06


def dequantize(quantized, scales, block_size):
    widened = jnp.repeat(jnp.repeat(scales, block_size, axis=0), block_size, axis=1)
    return (quantized.astype(jnp.float32) * widened).astype(jnp.bfloat16)


def shards(tokens, norm_gain, routes, gates, placement, w_in, in_scale, w_out, out_scale):
    tok_count = tokens.shape[0]
    width = tokens.shape[1]
    fanout = routes.shape[2]
    experts_all = placement.shape[1]
    capacity = max(2, 3 * tok_count * fanout // (2 * experts_all))
    hidden_width = w_out.shape[2]
    expert_ids = jnp.arange(experts_all, dtype=jnp.int32)
    slot_ids = jnp.arange(experts_all * capacity, dtype=jnp.int32)
    stream = tokens
    for layer_index in range(w_in.shape[0]):
        stream_f = stream.astype(jnp.float32)
        normed = (
            stream_f
            * lax.rsqrt(jnp.mean(stream_f * stream_f, axis=-1, keepdims=True) + epsilon)
            * norm_gain[layer_index]
        ).astype(jnp.bfloat16)
        in_weight = dequantize(w_in[layer_index, 0], in_scale[layer_index, 0], QBLK)
        out_weight = dequantize(w_out[layer_index, 0], out_scale[layer_index, 0], QBLK)
        matches = (placement[layer_index][:, None] == expert_ids[None, :]).astype(jnp.int32)
        holder = jnp.sum(matches * expert_ids[:, None], axis=0)
        chosen = routes[layer_index].reshape(-1)
        onehot = (chosen[:, None] == expert_ids[None, :]).astype(jnp.int32)
        ranks = jnp.sum((jnp.cumsum(onehot, axis=0) - 1) * onehot, axis=1)
        target = jnp.sum(onehot * holder[None, :], axis=1)
        slot_rows = target * capacity + ranks
        selector = (slot_rows[:, None] == slot_ids[None, :]).astype(jnp.bfloat16)
        spread = jnp.sum(
            selector.reshape(tok_count, fanout, -1).astype(jnp.float32), axis=1
        ).astype(jnp.bfloat16)
        outgoing = lax.dot_general(
            spread, normed, (((0,), (0,)), ((), ())), preferred_element_type=jnp.float32
        ).astype(jnp.bfloat16)
        outgoing = outgoing.reshape(experts_all, capacity, width)
        arrived = lax.all_to_all(
            outgoing, ("dp", "expert"), split_axis=0, concat_axis=0, tiled=True
        )
        arrived_shape = arrived.shape
        token_rows = arrived.reshape(-1, width)
        gate_up = jnp.dot(token_rows, in_weight, preferred_element_type=jnp.float32)
        hidden = (jax.nn.silu(gate_up[:, :hidden_width]) * gate_up[:, hidden_width:]).astype(
            jnp.bfloat16
        )
        answer = jnp.dot(hidden, out_weight, preferred_element_type=jnp.float32).astype(
            jnp.bfloat16
        )
        returned = lax.all_to_all(
            answer.reshape(arrived_shape), ("dp", "expert"), split_axis=0, concat_axis=0, tiled=True
        )
        back_rows = jnp.dot(
            selector, returned.reshape(-1, width), preferred_element_type=jnp.float32
        )
        back_rows = back_rows.reshape(tok_count, fanout, width)
        mixed = jnp.sum(back_rows * gates[layer_index][:, :, None], axis=1)
        stream = (stream_f + mixed).astype(jnp.bfloat16)
    return stream


GZ, GX, GY, GA, GB, GC, RC, RA, RB, RX, RY, RZ = range(12)


def moe_kernel(
    layers, experts_all, tok_ref, gain_ref, wts_ref, isc_ref, osc_ref, win_hbm, wout_hbm, out_ref,
    rows, win, wout, hid, part, acc, core_in, diag_out, diag_in, side_out, side_in, z_out, z_in,
    w_sem, send_sem, recv_sem,
):
    count, width = tok_ref.shape
    full = width + 128
    half = width // 2
    ff = wout.shape[1]
    z = lax.axis_index("dp")
    e = lax.axis_index("expert")
    c = e % 2
    q = e // 2
    x = q % 2
    y = q // 2
    xq = q + 1 - 2 * x
    yq = q + 2 - 4 * y
    dq = 3 - q
    dev_x = (z, e + 2 - 4 * x)
    dev_y = (z, e + 4 - 8 * y)
    dev_c = (z, e + 1 - 2 * c)

    def plane(k):
        return (z % 2 + k % 2) % 2 + 2 * ((z // 2 + k // 2) % 2)

    for l in range(layers):
        pltpu.make_async_copy(win_hbm.at[l, 0], win.at[l], w_sem.at[l, 0]).start()
        pltpu.make_async_copy(wout_hbm.at[l, 0], wout.at[l], w_sem.at[l, 1]).start()

    barrier = pltpu.get_barrier_semaphore()
    partners = [dev_x, dev_y, dev_c] + [(plane(k), e) for k in range(1, 4)]
    for dev in partners:
        pl.semaphore_signal(barrier, inc=1, device_id=dev, device_id_type=MESH)
    pl.semaphore_wait(barrier, len(partners))

    def scale_in(l, lo, hi):
        @pl.loop(lo * 4, hi * 4)
        def _(i):
            r = pl.ds(pl.multiple_of(i * 32, 32), 32)
            win[l, r, :] = (win[l, r, :].astype(jnp.float32) * isc_ref[l, pl.ds(i // 4, 1), :]).astype(jnp.bfloat16)

    def scale_out(l):
        @pl.loop(0, ff // 32)
        def _(i):
            r = pl.ds(pl.multiple_of(i * 32, 32), 32)
            wout[l, r, :] = (wout[l, r, :].astype(jnp.float32) * osc_ref[l, pl.ds(i // 4, 1), :]).astype(jnp.bfloat16)

    blocks = win.shape[1] // QBLK

    def dequant(l, step):
        if step == 0:
            pltpu.make_async_copy(win_hbm.at[l, 0], win.at[l], w_sem.at[l, 0]).wait()
            scale_in(l, 0, blocks // 2)
        elif step == 1:
            scale_in(l, blocks // 2, blocks)
        else:
            pltpu.make_async_copy(wout_hbm.at[l, 0], wout.at[l], w_sem.at[l, 1]).wait()
            scale_out(l)

    acc[...] = tok_ref[...].astype(jnp.float32)

    def layer(l, carry):
        sent = []

        def copy(src, dst, k, kind, dev):
            return pltpu.make_async_remote_copy(
                src_ref=src, dst_ref=dst,
                send_sem=send_sem.at[l, k, kind], recv_sem=recv_sem.at[l, k, kind],
                device_id=dev, device_id_type=MESH,
            )

        def start(src, dst, k, kind, dev):
            op = copy(src, dst, k, kind, dev)
            op.start()
            sent.append(op)

        def arrived(dst, k, kind, dev):
            copy(dst, dst, k, kind, dev).wait_recv()

        left, right = pl.ds(0, half), pl.ds(half, full - half)

        def shard(k, place):
            return rows.at[l, plane(k), c, place]

        def g1(k):
            mine = shard(k, q)
            if k > 0:
                arrived(mine, k, GZ, (plane(k), e))
            start(mine, mine, k, GX, dev_x)
            start(mine, mine, k, GY, dev_y)

        def g2(k):
            arrived(shard(k, xq), k, GX, dev_x)
            piece = rows.at[l, plane(k), c, xq, :, left]
            start(piece, piece, k, GA, dev_y)
            arrived(shard(k, yq), k, GY, dev_y)
            piece = rows.at[l, plane(k), c, yq, :, right]
            start(piece, piece, k, GB, dev_x)

        def g3(k):
            arrived(rows.at[l, plane(k), c, dq, :, left], k, GA, dev_y)
            arrived(rows.at[l, plane(k), c, dq, :, right], k, GB, dev_x)
            ours = rows.at[l, plane(k), c]
            start(ours, ours, k, GC, dev_c)

        def compute(k):
            arrived(rows.at[l, plane(k), 1 - c], k, GC, dev_c)
            zk = plane(k)
            total = 8 * count
            picks = rows[l, zk, :, :, :, width:].reshape(total, full - width).astype(jnp.float32)
            lane = lax.broadcasted_iota(jnp.int32, picks.shape, 1)
            me = z * 8 + e
            own = (lane == me) | (lane == me + experts_all)
            weight = jnp.sum(jnp.where(own, picks, 0.0), axis=1, keepdims=True)

            @pl.loop(0, ff // 256, unroll=True)
            def _(j):
                data = rows[l, zk, :, :, :, :width].reshape(total, width)
                g_cols = pl.ds(pl.multiple_of(j * 256, 256), 256)
                u_cols = pl.ds(pl.multiple_of(ff + j * 256, 256), 256)
                gate = jnp.dot(data, win[l, :, g_cols], preferred_element_type=jnp.float32)
                up = jnp.dot(data, win[l, :, u_cols], preferred_element_type=jnp.float32)
                hid[:, g_cols] = (gate / (1.0 + jnp.exp(-gate)) * up).astype(jnp.bfloat16)

            @pl.loop(0, width // 512)
            def _(j):
                cols = pl.ds(pl.multiple_of(j * 512, 512), 512)
                answer = jnp.dot(hid[...], wout[l, :, cols], preferred_element_type=jnp.float32)
                answer = answer.astype(jnp.bfloat16).astype(jnp.float32) * weight
                part[k, :, :, :, cols] = answer.astype(jnp.bfloat16).reshape(2, 4, count, 512)

            start(part.at[k, 1 - c], core_in.at[l, k], k, RC, dev_c)

        def chip_sum(k, place):
            return part[k, c, place].astype(jnp.float32) + core_in[l, k, place].astype(jnp.float32)

        def r2(k):
            arrived(core_in.at[l, k], k, RC, dev_c)
            far = chip_sum(k, dq).astype(jnp.bfloat16)
            diag_out[k, 0] = far[:, :half]
            diag_out[k, 1] = far[:, half:]
            start(diag_out.at[k, 0], diag_in.at[l, k, 0], k, RA, dev_x)
            start(diag_out.at[k, 1], diag_in.at[l, k, 1], k, RB, dev_y)

        def r3(k):
            arrived(diag_in.at[l, k, 1], k, RB, dev_y)
            near = chip_sum(k, xq)
            side_out[k, 0, :, :half] = near[:, :half].astype(jnp.bfloat16)
            side_out[k, 0, :, half:] = (near[:, half:] + diag_in[l, k, 1].astype(jnp.float32)).astype(jnp.bfloat16)
            start(side_out.at[k, 0], side_in.at[l, k, 0], k, RX, dev_x)
            arrived(diag_in.at[l, k, 0], k, RA, dev_x)
            near = chip_sum(k, yq)
            side_out[k, 1, :, :half] = (near[:, :half] + diag_in[l, k, 0].astype(jnp.float32)).astype(jnp.bfloat16)
            side_out[k, 1, :, half:] = near[:, half:].astype(jnp.bfloat16)
            start(side_out.at[k, 1], side_in.at[l, k, 1], k, RY, dev_y)

        def r4(k):
            arrived(side_in.at[l, k, 0], k, RX, dev_x)
            arrived(side_in.at[l, k, 1], k, RY, dev_y)
            whole = chip_sum(k, q) + side_in[l, k, 0].astype(jnp.float32) + side_in[l, k, 1].astype(jnp.float32)
            if k == 0:
                acc[...] += whole
            else:
                z_out[k] = whole.astype(jnp.bfloat16)
                start(z_out.at[k], z_in.at[l, k], k, RZ, (plane(k), e))

        stream = acc[...]
        inverse = lax.rsqrt(jnp.mean(stream * stream, axis=-1, keepdims=True) + epsilon)
        rows[l, z, c, q, :, :width] = (stream * inverse * gain_ref[pl.ds(l, 1), :]).astype(jnp.bfloat16)
        rows[l, z, c, q, :, width:] = wts_ref[l]
        mine = rows.at[l, z, c, q]
        g1(0)
        for k in range(1, 4):
            start(mine, mine, k, GZ, (plane(k), e))

        def ahead(step):
            @pl.when(l + 1 < layers)
            def _():
                dequant(l + 1, step)

        @pl.when(l == 0)
        def _():
            dequant(0, 0)

        g2(0), g1(1)

        @pl.when(l == 0)
        def _():
            dequant(0, 1)

        g3(0), g2(1), g1(2)

        @pl.when(l == 0)
        def _():
            dequant(0, 2)

        compute(0), g3(1), g2(2), g1(3)
        compute(1), r2(0), g3(2), g2(3)
        compute(2), r3(0), r2(1), g3(3)
        compute(3), r4(0), r3(1), r2(2)
        ahead(0)
        r4(1), r3(2), r2(3)
        ahead(1)
        r4(2), r3(3)
        ahead(2)
        r4(3)
        for k in range(1, 4):
            arrived(z_in.at[l, k], k, RZ, (plane(k), e))
            acc[...] += z_in[l, k].astype(jnp.float32)
        acc[...] = acc[...].astype(jnp.bfloat16).astype(jnp.float32)
        for op in sent:
            op.wait_send()
        return carry

    lax.fori_loop(0, layers, layer, 0)
    out_ref[...] = acc[...].astype(jnp.bfloat16)


def fused(tokens, norm_gain, routes, gates, placement, w_in, in_scale, w_out, out_scale):
    count, width = tokens.shape
    layers = w_in.shape[0]
    ff = w_out.shape[2]
    chosen = routes[:, :, :, None] == placement[:, None, None, :]
    share = jnp.sum(jnp.where(chosen, gates[:, :, :, None], 0.0), axis=2)
    high = lax.reduce_precision(share, 8, 7)
    low = share - high
    wts = jnp.concatenate([high, low, jnp.zeros_like(high), jnp.zeros_like(high)], axis=-1)
    wts = wts.astype(jnp.bfloat16)
    isc = jnp.repeat(in_scale[:, 0], QBLK, axis=2)
    osc = jnp.repeat(out_scale[:, 0], QBLK, axis=2)
    vmem = pl.BlockSpec(memory_space=pltpu.VMEM)
    hbm = pl.BlockSpec(memory_space=pl.ANY)
    b16 = jnp.bfloat16
    return pl.pallas_call(
        functools.partial(moe_kernel, layers, placement.shape[1]),
        out_shape=jax.ShapeDtypeStruct((count, width), b16),
        in_specs=[vmem] * 5 + [hbm] * 2,
        out_specs=vmem,
        scratch_shapes=[
            pltpu.VMEM((layers, 4, 2, 4, count, width + 128), b16),
            pltpu.VMEM((layers, width, 2 * ff), b16),
            pltpu.VMEM((layers, ff, width), b16),
            pltpu.VMEM((8 * count, ff), b16),
            pltpu.VMEM((4, 2, 4, count, width), b16),
            pltpu.VMEM((count, width), jnp.float32),
            pltpu.VMEM((layers, 4, 4, count, width), b16),
            pltpu.VMEM((4, 2, count, width // 2), b16),
            pltpu.VMEM((layers, 4, 2, count, width // 2), b16),
            pltpu.VMEM((4, 2, count, width), b16),
            pltpu.VMEM((layers, 4, 2, count, width), b16),
            pltpu.VMEM((4, count, width), b16),
            pltpu.VMEM((layers, 4, count, width), b16),
            pltpu.SemaphoreType.DMA((layers, 2)),
            pltpu.SemaphoreType.DMA((layers, 4, 12)),
            pltpu.SemaphoreType.DMA((layers, 4, 12)),
        ],
        compiler_params=pltpu.CompilerParams(
            collective_id=0, has_side_effects=True, vmem_limit_bytes=58 * 1024 * 1024
        ),
    )(tokens, norm_gain, wts, isc, osc, w_in, w_out)


def solution(mesh):
    fits = mesh.shape["dp"] == 4 and mesh.shape["expert"] == 8
    return jax.shard_map(
        fused if fits else shards,
        mesh=mesh,
        in_specs=(
            P(("dp", "expert"), None),
            P(),
            P(None, ("dp", "expert"), None),
            P(None, ("dp", "expert"), None),
            P(),
            P(None, ("dp", "expert"), None, None),
            P(None, ("dp", "expert"), None, None),
            P(None, ("dp", "expert"), None, None),
            P(None, ("dp", "expert"), None, None),
        ),
        out_specs=P(("dp", "expert"), None),
        check_vma=False,
    )
```
